256 devices in a mesh: task: 4 (over y), row: 64 (over x, z, core).
Axes of the slice: x: 4, y: 4, z: 8, core: 2. Of those that a mesh axis runs over, the one named last changes fastest.
Arguments:
- u_basis: bfloat16 [8192, 1024], P('row', 'task'), may hold values from -8.838835 to 8.838835
- v_basis: bfloat16 [28672, 1024], P('row', 'task'), may hold values from -4.724556 to 4.724556
- singular: float32 [1024], replicated, may hold values from 100 to 1000
- ranks: int32 [16], replicated, may hold values from 1 to 64, 768 in all
Outputs:
- delta: bfloat16 [8192, 28672], P('task', 'row')
The draws below stay inside these ranges and needn't reach their ends.
Inputs may be any that keep to these rules, and one draw needn't show every extreme that they name: ranks sum to 768.
All inputs are finite; a program needn't handle non-finite values.
Results may differ from the reference program's by a relative error of at most 0.0057.
Values may be sent and summed in bfloat16 or wider, within the bound.
No kernel may reach another device: no remote copies, remote signals or barrier semaphores. Data moves between devices by JAX's collectives and lax.ppermute only.
A program may use at most 128 MiB of HBM per device.

```python
import math
import jax
import jax.numpy as jnp
import numpy as np
from jax import lax

D = 8192
FF = 28672
CAP = 64
ITERS = 3
TASKS = 16
RANK_SUM = 768


def factor_draw(key, rows, cols):
    keys = jax.random.split(key, 5)
    noise = jax.random.normal(keys[0], (rows, cols), jnp.float32)
    col_scale = jnp.exp(jax.random.uniform(keys[3], (1, cols), jnp.float32) * math.log(10.0))
    row_scale = jnp.exp(jax.random.uniform(keys[4], (rows, 1), jnp.float32) * math.log(10.0))
    value = noise * col_scale * row_scale / math.sqrt(rows)
    limit = 800.0 / math.sqrt(rows)
    return jnp.clip(value, -limit, limit).astype(jnp.bfloat16)


def draw_u_basis(key, part):
    key = jax.random.fold_in(key, 11)
    return factor_draw(key, D, TASKS * CAP)


def draw_v_basis(key, part):
    key = jax.random.fold_in(key, 23)
    return factor_draw(key, FF, TASKS * CAP)


def length_profile(number_of, total, most, slope):
    loads = [(1 << 20) // math.isqrt(grade ** slope) + 1 for grade in range(2, number_of + 1)]
    surplus, counts = total - most - (number_of - 1), [1] * (number_of - 1)
    while surplus > 0:
        free = [i for i in range(number_of - 1) if counts[i] < most]
        pool, left = sum([loads[i] for i in free]), surplus
        for i in free:
            extra = min(most - counts[i], max(1, left * loads[i] // pool), surplus)
            counts[i] = counts[i] + extra
            surplus = surplus - extra
    return np.array([most] + counts)


def ragged(stream_key, count, total, most, lean):
    if count == 2:
        one = jax.random.randint(stream_key, (), max(1, total - most), min(most, total - 1) + 1)
        return jnp.stack([one, total - one])
    lengths = jnp.asarray(length_profile(count, total, most, lean), jnp.int32)
    couples = (count - 1) // 2
    giver, sink = lengths[1:1 + 2 * couples:2], lengths[2:2 + 2 * couples:2]
    slack = jnp.minimum(giver - 1, most - sink)
    passed = jax.random.randint(jax.random.fold_in(stream_key, 1), (couples,), 0, 1 << 20) % (slack + 1)
    lengths = lengths.at[1:1 + 2 * couples:2].set(giver - passed).at[2:2 + 2 * couples:2].set(sink + passed)
    return lengths[jax.random.permutation(jax.random.fold_in(stream_key, 2), count)]


def setup_inputs(seed: int = 0) -> dict:
    seeds = jax.random.split(jax.random.key(seed), 5)
    return {
        "u_basis": draw_u_basis(jax.random.fold_in(seeds[4], 71), 0),
        "v_basis": draw_v_basis(jax.random.fold_in(seeds[4], 71), 0),
        "singular": jnp.clip(jnp.exp(jax.random.uniform(seeds[2], (TASKS * CAP,), jnp.float32, math.log(100.0), math.log(1000.0))), 100.0, 1000.0),
        "ranks": ragged(seeds[3], TASKS, RANK_SUM, CAP, 2).astype(jnp.int32),
    }


def whiten(basis):
    gram = jnp.dot(basis.T, basis, precision=lax.Precision.HIGHEST, preferred_element_type=jnp.float32)
    frob = jnp.sqrt(jnp.sum(gram * gram))
    basis = basis / jnp.sqrt(frob)
    inner = gram / frob
    basis = 1.5 * basis - 0.5 * jnp.dot(basis, inner, precision=lax.Precision.HIGHEST, preferred_element_type=jnp.float32)
    for step in range(1, ITERS):
        inner = jnp.dot(basis.T, basis, precision=lax.Precision.HIGHEST, preferred_element_type=jnp.float32)
        basis = 1.5 * basis - 0.5 * jnp.dot(basis, inner, precision=lax.Precision.HIGHEST, preferred_element_type=jnp.float32)
    return basis

def reference(u_basis, v_basis, singular, ranks):
    live = (jnp.arange(CAP, dtype=jnp.int32)[None, :] < ranks[:, None]).reshape(-1).astype(jnp.float32)
    u_white = whiten(u_basis.astype(jnp.float32) * live)
    v_white = whiten(v_basis.astype(jnp.float32) * live)
    u_round = u_white.astype(jnp.bfloat16)
    weighted = (v_white * singular[None, :]).astype(jnp.bfloat16)
    blocks = u_round.reshape(8, D // 8, u_round.shape[1])

    def rebuild(rows):
        return jnp.dot(rows, weighted.T, preferred_element_type=jnp.float32).astype(jnp.bfloat16)
    return lax.map(rebuild, blocks).reshape(D, FF)
```

```python
import functools
import math

import jax
import jax.numpy as jnp
from jax import lax
from jax.experimental import pallas as pl
from jax.experimental.pallas import tpu as pltpu
from jax.sharding import Mesh, PartitionSpec as P

BF = jnp.bfloat16
F32 = jnp.float32
LIVE = 768
SIDE = 256
HALF = 128
PAIRS = ((0, 0), (0, 1), (0, 2), (1, 1), (1, 2), (2, 2))


def select_matrix(ranks_ref, sel, tasks, cap):
    row = lax.broadcasted_iota(jnp.int32, (cap, LIVE), 0)
    col = lax.broadcasted_iota(jnp.int32, (cap, LIVE), 1)
    diff = col - row
    offset = jnp.int32(0)
    for t in range(tasks):
        rank = ranks_ref[t]
        hit = (diff == offset) & (row < rank)
        sel[t * cap : (t + 1) * cap, :] = jnp.where(hit, 1.0, 0.0).astype(BF)
        offset = offset + rank


def gram_kernel(tasks, cap, rows_u, place_ref, ranks_ref, x_ref, part_ref, right_ref, sel_ref, xc):
    select_matrix(ranks_ref, sel_ref, tasks, cap)
    shards, rows, width = x_ref.shape
    total = jnp.zeros((rows, LIVE), F32)
    for s in range(shards):
        total += jnp.dot(x_ref[s], sel_ref[s * width : (s + 1) * width, :], preferred_element_type=F32)
    xc[...] = total.astype(BF)
    right_ref[...] = xc[rows_u:, :]
    place = place_ref[0]

    for y in range(4):

        @pl.when(place == y)
        def _():
            base = xc[:rows_u, :] if y < 2 else xc[rows_u:, :]
            for b in range(3):
                i, j = PAIRS[(y % 2) * 3 + b]
                block = lax.dot_general(
                    base[:, i * SIDE : (i + 1) * SIDE],
                    base[:, j * SIDE : (j + 1) * SIDE],
                    (((0,), (0,)), ((), ())),
                    preferred_element_type=F32,
                ).astype(BF)
                for h in range(2):
                    part_ref[(b * 2 + h) * SIDE : (b * 2 + h + 1) * SIDE, :] = block[:, h * HALF : (h + 1) * HALF]


def load_gram(gram_ref, side, full):
    square = jnp.float32(0)
    blocks = []
    for p, (i, j) in enumerate(PAIRS):
        y, b = side * 2 + p // 3, p % 3
        for h in range(2):
            hb = b * 2 + h
            block = gram_ref[hb // 3, y, hb % 3].astype(F32)
            square += jnp.sum(block * block) * (1.0 if i == j else 2.0)
            blocks.append((i, j, h, block))
    norm = jnp.sqrt(jnp.full((1, 1), square, F32))
    inverse = 1.0 / norm
    for i, j, h, block in blocks:
        scaled = block * inverse
        full[i * SIDE : (i + 1) * SIDE, j * SIDE + h * HALF : j * SIDE + (h + 1) * HALF] = scaled.astype(BF)
        if i != j:
            full[j * SIDE + h * HALF : j * SIDE + (h + 1) * HALF, i * SIDE : (i + 1) * SIDE] = scaled.T.astype(BF)
    return norm


def mm(a, b):
    return jnp.dot(a.astype(BF), b, preferred_element_type=F32)


def whiten_rows(x, a0, a1, tmp):
    tmp[...] = mm(a0[...], a0[...]).astype(BF)
    cube = mm(tmp[...], a0[...])
    a1[...] = (2.25 * a0[...].astype(F32) - 1.5 * tmp[...].astype(F32) + 0.25 * cube).astype(BF)
    x = 1.5 * x - 0.5 * mm(x, a0[...])
    t = mm(x, a1[...])
    x = 1.5 * x - 0.5 * t
    t = mm(x, a1[...])
    t = 1.5 * t - 0.5 * mm(t, a1[...])
    t = 1.5 * t - 0.5 * mm(t, a1[...])
    return 1.5 * x - 0.5 * t


def weight_kernel(gram_ref, right_ref, values_ref, sel_ref, out_ref, a0, a1, tmp):
    norm_v = load_gram(gram_ref, 1, a0)
    w = whiten_rows(right_ref[...].astype(F32), a0, a1, tmp)
    values = lax.dot_general(
        values_ref[...], sel_ref[...].astype(F32), (((1,), (0,)), ((), ())),
        precision=lax.Precision.HIGHEST, preferred_element_type=F32,
    )
    w = w * values
    norm_u = load_gram(gram_ref, 0, a0)
    w = whiten_rows(w, a0, a1, tmp)
    w = w * (lax.rsqrt(norm_v) * lax.rsqrt(norm_u))
    out_ref[...] = lax.dot_general(
        w.astype(BF), sel_ref[...], (((1,), (1,)), ((), ())), preferred_element_type=F32
    ).astype(BF)


def product_kernel(u_ref, w_ref, out_ref):
    shards, _, width = u_ref.shape
    total = None
    for s in range(shards):
        part = lax.dot_general(
            u_ref[s], w_ref[:, s * width : (s + 1) * width], (((1,), (1,)), ((), ())), preferred_element_type=F32
        )
        total = part if total is None else total + part
    out_ref[...] = total.astype(BF)


def on_device(u_basis, v_basis, singular, ranks):
    tasks = ranks.shape[0]
    columns = singular.shape[0]
    cap = columns // tasks
    rows_u, width = u_basis.shape
    rows_v = v_basis.shape[0]
    ny, nx, nz, nc = (lax.axis_size(a) for a in ("y", "x", "z", "c"))
    place = lax.axis_index("y")

    swap = [(a * nx + b, b * nx + a) for a in range(ny) for b in range(nx)]
    turned = lax.ppermute(u_basis, ("y", "x"), swap)
    left = lax.all_gather(turned, ("x", "z", "c"))
    left = left.reshape(nx, nz * nc * rows_u, width)

    both = jnp.concatenate([u_basis, v_basis])
    both = jnp.broadcast_to(both[None], (ny,) + both.shape)
    full = lax.all_to_all(both, "y", 0, 0)

    vmem = pl.BlockSpec(memory_space=pltpu.VMEM)
    smem = pl.BlockSpec(memory_space=pltpu.SMEM)
    pieces = 6 * SIDE
    part, right, sel = pl.pallas_call(
        functools.partial(gram_kernel, tasks, cap, rows_u),
        out_shape=(
            jax.ShapeDtypeStruct((pieces, HALF), BF),
            jax.ShapeDtypeStruct((rows_v, LIVE), BF),
            jax.ShapeDtypeStruct((columns, LIVE), BF),
        ),
        in_specs=[smem, smem, vmem],
        out_specs=(vmem, vmem, vmem),
        scratch_shapes=[pltpu.VMEM((rows_u + rows_v, LIVE), BF)],
        compiler_params=pltpu.CompilerParams(vmem_limit_bytes=48 << 20),
        name="gram",
    )(place.reshape(1), ranks, full)

    other = lax.ppermute(part, "c", [(0, 1), (1, 0)])
    half = part.shape[0] // nc
    start = lax.axis_index("c") * half
    mine = lax.dynamic_slice_in_dim(part, start, half).astype(F32)
    mine = mine + lax.dynamic_slice_in_dim(other, start, half).astype(F32)
    spread = lax.all_to_all(mine.astype(BF).reshape(nx * nz, half // (nx * nz), HALF), ("x", "z"), 0, 0)
    piece = jnp.sum(spread.astype(F32), axis=0).astype(BF)

    piece = lax.all_to_all(jnp.broadcast_to(piece[None], (nz,) + piece.shape), "z", 0, 0)
    piece = piece.reshape(-1, HALF)
    piece = lax.all_to_all(jnp.broadcast_to(piece[None], (ny * nx,) + piece.shape), ("y", "x"), 0, 0)
    gram = lax.all_gather(piece, "c").reshape(nc, ny, 3, SIDE, HALF)

    weight = pl.pallas_call(
        weight_kernel,
        out_shape=jax.ShapeDtypeStruct((rows_v, columns), BF),
        in_specs=[vmem] * 4,
        out_specs=vmem,
        scratch_shapes=[pltpu.VMEM((LIVE, LIVE), BF)] * 3,
        compiler_params=pltpu.CompilerParams(vmem_limit_bytes=56 << 20),
        name="weight",
    )(gram, right, singular.reshape(1, columns), sel)

    tile = 256
    rows = left.shape[1]
    return pl.pallas_call(
        product_kernel,
        grid=(rows // tile,),
        out_shape=jax.ShapeDtypeStruct((rows, rows_v), BF),
        in_specs=[
            pl.BlockSpec((nx, tile, width), lambda i: (0, i, 0)),
            pl.BlockSpec((rows_v, columns), lambda i: (0, 0)),
        ],
        out_specs=pl.BlockSpec((tile, rows_v), lambda i: (i, 0)),
        compiler_params=pltpu.CompilerParams(vmem_limit_bytes=32 << 20),
        name="product",
    )(left, weight)


def solution(mesh):
    grid = Mesh(mesh.devices.reshape(4, 4, 8, 2), ("y", "x", "z", "c"))
    row = ("x", "z", "c")
    return jax.shard_map(
        on_device,
        mesh=grid,
        in_specs=(P(row, "y"), P(row, "y"), P(), P()),
        out_specs=P("y", row),
        check_vma=False,
    )
```

```python
import functools

import jax
import jax.numpy as jnp
from jax import lax
from jax.experimental import pallas as pl
from jax.experimental.pallas import tpu as pltpu
from jax.sharding import Mesh, PartitionSpec as P

BF = jnp.bfloat16
F32 = jnp.float32
LIVE = 768
SIDE = 256
HALF = 128
PAIRS = ((0, 0), (0, 1), (0, 2), (1, 1), (1, 2), (2, 2))


def select_matrix(ranks_ref, values_ref, sel, live_values, tasks, cap):
    row = lax.broadcasted_iota(jnp.int32, (cap, LIVE), 0)
    col = lax.broadcasted_iota(jnp.int32, (cap, LIVE), 1)
    diff = col - row
    offset = jnp.int32(0)
    upright = values_ref[...].T
    per_row = values_ref.shape[1] // cap
    picked = jnp.zeros((cap, LIVE), F32)
    for t in range(tasks):
        rank = ranks_ref[t]
        hit = (diff == offset) & (row < rank)
        sel[t * cap : (t + 1) * cap, :] = jnp.where(hit, 1.0, 0.0).astype(BF)
        at = t % per_row * cap
        column = upright[at : at + cap, t // per_row : t // per_row + 1]
        picked += jnp.where(hit, column, 0.0)
        offset = offset + rank
    live_values[...] = jnp.sum(picked, axis=0, keepdims=True)


def prepare_kernel(tasks, cap, ranks_ref, values_ref, u_ref, v_ref, stack_ref, sel_ref, live_ref, sems):
    shards, rows_u = stack_ref.shape[0], u_ref.shape[0]
    copies = []
    for s in range(shards):
        copies.append(pltpu.make_async_copy(u_ref, stack_ref.at[s, pl.ds(0, rows_u), :], sems.at[0, s]))
        copies.append(pltpu.make_async_copy(v_ref, stack_ref.at[s, pl.ds(rows_u, v_ref.shape[0]), :], sems.at[1, s]))
    for copy in copies:
        copy.start()
    select_matrix(ranks_ref, values_ref, sel_ref, live_ref, tasks, cap)
    for copy in copies:
        copy.wait()


def gram_kernel(rows_u, place_ref, core_ref, x_ref, sel, keep_ref, give_ref, right_ref, sel_ref, right, left, sems):
    shards = x_ref.shape[0]
    save_sel = pltpu.make_async_copy(sel, sel_ref, sems.at[0])
    save_sel.start()
    width = x_ref.shape[2]
    place, core = place_ref[0], core_ref[0]
    total = None
    for s in range(shards):
        part = jnp.dot(x_ref[s, rows_u:, :], sel[s * width : (s + 1) * width, :], preferred_element_type=F32)
        total = part if total is None else total + part
    right[...] = total.astype(BF)
    save_right = pltpu.make_async_copy(right, right_ref, sems.at[1])
    save_right.start()

    @pl.when(place < 2)
    def _():
        total = None
        for s in range(shards):
            part = jnp.dot(x_ref[s, :rows_u, :], sel[s * width : (s + 1) * width, :], preferred_element_type=F32)
            total = part if total is None else total + part
        left[...] = total.astype(BF)

    for y in range(shards):

        @pl.when(place == y)
        def _():
            base = left if y < 2 else right
            for b in range(3):
                i, j = PAIRS[(y % 2) * 3 + b]
                block = lax.dot_general(
                    base[:, i * SIDE : (i + 1) * SIDE],
                    base[:, j * SIDE : (j + 1) * SIDE],
                    (((0,), (0,)), ((), ())),
                    preferred_element_type=F32,
                )
                for h in range(2):
                    c, k = divmod(b * 2 + h, 3)
                    half = block[:, h * HALF : (h + 1) * HALF]

                    @pl.when(core == c)
                    def _():
                        keep_ref[k * SIDE : (k + 1) * SIDE, :] = half

                    @pl.when(core != c)
                    def _():
                        give_ref[k * SIDE : (k + 1) * SIDE, :] = half.astype(BF)

    save_sel.wait()
    save_right.wait()


def load_gram(core, own_ref, other_ref, side, full):
    square = jnp.zeros((1, 1), F32)
    blocks = []
    for p, (i, j) in enumerate(PAIRS):
        y, b = side * 2 + p // 3, p % 3
        for h in range(2):
            c, k = divmod(b * 2 + h, 3)
            block = jnp.where(core == c, own_ref[y, k].astype(F32), other_ref[y, k].astype(F32))
            square += jnp.sum(block * block, keepdims=True) * (1.0 if i == j else 2.0)
            blocks.append((i, j, h, block))
    norm = jnp.sqrt(square)
    inverse = 1.0 / norm
    for i, j, h, block in blocks:
        scaled = block * inverse
        full[i * SIDE : (i + 1) * SIDE, j * SIDE + h * HALF : j * SIDE + (h + 1) * HALF] = scaled.astype(BF)
        if i != j:
            full[j * SIDE + h * HALF : j * SIDE + (h + 1) * HALF, i * SIDE : (i + 1) * SIDE] = scaled.T.astype(BF)
    return norm


def mm(a, b):
    return jnp.dot(a.astype(BF), b, preferred_element_type=F32)


def whiten_rows(x, a0, a1, tmp):
    tmp[...] = mm(a0[...], a0[...]).astype(BF)
    cube = mm(tmp[...], a0[...])
    a1[...] = (2.25 * a0[...].astype(F32) - 1.5 * tmp[...].astype(F32) + 0.25 * cube).astype(BF)
    x = 1.5 * x - 0.5 * mm(x, a0[...])
    t = mm(x, a1[...])
    x = 1.5 * x - 0.5 * t
    t = mm(x, a1[...])
    t = 1.5 * t - 0.5 * mm(t, a1[...])
    t = 1.5 * t - 0.5 * mm(t, a1[...])
    return 1.5 * x - 0.5 * t


def weight_kernel(core_ref, own_ref, other_ref, right_ref, live_ref, sel_ref, out_ref, a0, a1, tmp, right, sel, sems):
    load_right = pltpu.make_async_copy(right_ref, right, sems.at[0])
    load_sel = pltpu.make_async_copy(sel_ref, sel, sems.at[1])
    load_right.start()
    load_sel.start()
    core = core_ref[0]
    norm_v = load_gram(core, own_ref, other_ref, 1, a0)
    load_right.wait()
    w = whiten_rows(right[...].astype(F32), a0, a1, tmp)
    w = w * live_ref[...]
    norm_u = load_gram(core, own_ref, other_ref, 0, a0)
    w = whiten_rows(w, a0, a1, tmp)
    w = w * (lax.rsqrt(norm_v) * lax.rsqrt(norm_u))
    load_sel.wait()
    out_ref[...] = lax.dot_general(
        w.astype(BF), sel[...], (((1,), (1,)), ((), ())), preferred_element_type=F32
    ).astype(BF)


def product_kernel(plan, w_ref, left_ref, out_ref, left, out, in_sem, out_sem):
    shards, _, width = left.shape
    spans = [(sum(plan[:i]), n) for i, n in enumerate(plan)]
    fetch = [
        pltpu.make_async_copy(left_ref.at[:, pl.ds(a, n), :], left.at[:, pl.ds(a, n), :], in_sem.at[i])
        for i, (a, n) in enumerate(spans)
    ]
    for copy in fetch:
        copy.start()
    store = []
    for i, (a, n) in enumerate(spans):
        fetch[i].wait()
        total = None
        for s in range(shards):
            part = lax.dot_general(
                w_ref[:, s * width : (s + 1) * width],
                left[s, a : a + n, :],
                (((1,), (1,)), ((), ())),
                preferred_element_type=F32,
            )
            total = part if total is None else total + part
        out[:, a : a + n] = total.astype(BF)
        store.append(pltpu.make_async_copy(out.at[:, pl.ds(a, n)], out_ref.at[:, pl.ds(a, n)], out_sem.at[i]))
        store[i].start()
    for copy in store:
        copy.wait()


def on_device(u_basis, v_basis, singular, ranks):
    tasks = ranks.shape[0]
    columns = singular.shape[0]
    cap = columns // tasks
    rows_u, width = u_basis.shape
    rows_v = v_basis.shape[0]
    ny, nx, nz, nc = (lax.axis_size(a) for a in ("y", "x", "z", "c"))
    place = lax.axis_index("y")
    core = lax.axis_index("c")
    vmem = pl.BlockSpec(memory_space=pltpu.VMEM)
    smem = pl.BlockSpec(memory_space=pltpu.SMEM)
    hbm = pl.BlockSpec(memory_space=pltpu.HBM)
    in_hbm = lambda a: pltpu.with_memory_space_constraint(a, pltpu.HBM)

    swap = [(a * nx + b, b * nx + a) for a in range(ny) for b in range(nx)]
    turned = lax.ppermute(u_basis, ("y", "x"), swap)
    stack, sel, live = pl.pallas_call(
        functools.partial(prepare_kernel, tasks, cap),
        out_shape=(
            pltpu.HBM((ny, rows_u + rows_v, width), BF),
            jax.ShapeDtypeStruct((columns, LIVE), BF),
            jax.ShapeDtypeStruct((1, LIVE), F32),
        ),
        in_specs=[smem, vmem, vmem, vmem],
        out_specs=(hbm, vmem, vmem),
        scratch_shapes=[pltpu.SemaphoreType.DMA((2, ny))],
        compiler_params=pltpu.CompilerParams(vmem_limit_bytes=16 << 20),
        name="prepare",
    )(ranks, singular.reshape(columns // HALF, HALF), u_basis, v_basis)
    turned, stack, sel, live = lax.optimization_barrier((turned, stack, sel, live))
    left = lax.all_gather(turned, ("x", "z", "c"))
    left = left.reshape(nx, nz * nc * rows_u, width)

    full = lax.all_to_all(stack, "y", 0, 0)

    half = 3 * SIDE
    keep, give, right, saved_sel = pl.pallas_call(
        functools.partial(gram_kernel, rows_u),
        out_shape=(
            jax.ShapeDtypeStruct((half, HALF), F32),
            jax.ShapeDtypeStruct((half, HALF), BF),
            pltpu.HBM((rows_v, LIVE), BF),
            pltpu.HBM((columns, LIVE), BF),
        ),
        in_specs=[smem, smem, vmem, vmem],
        out_specs=(vmem, vmem, hbm, hbm),
        scratch_shapes=[
            pltpu.VMEM((rows_v, LIVE), BF),
            pltpu.VMEM((rows_u, LIVE), BF),
            pltpu.SemaphoreType.DMA((2,)),
        ],
        compiler_params=pltpu.CompilerParams(vmem_limit_bytes=24 << 20),
        cost_estimate=pl.CostEstimate(flops=1 << 30, bytes_accessed=4 << 20, transcendentals=0),
        name="gram",
    )(place.reshape(1), core.reshape(1), full, sel)

    swap_cores = [(0, 1), (1, 0)]
    mine = keep + lax.ppermute(give, "c", swap_cores).astype(F32)
    spread = lax.all_to_all(mine.astype(BF).reshape(nx * nz, half // (nx * nz), HALF), ("x", "z"), 0, 0)
    piece = jnp.sum(spread.astype(F32), axis=0).astype(BF)

    piece = lax.all_to_all(jnp.broadcast_to(piece[None], (nz,) + piece.shape), "z", 0, 0)
    piece = piece.reshape(-1, HALF)
    piece = lax.all_to_all(jnp.broadcast_to(piece[None], (ny * nx,) + piece.shape), ("y", "x"), 0, 0)
    piece = piece.reshape(ny, 3, SIDE, HALF)
    across = lax.ppermute(piece, "c", swap_cores)

    weight = pl.pallas_call(
        weight_kernel,
        out_shape=jax.ShapeDtypeStruct((rows_v, columns), BF),
        in_specs=[smem, vmem, vmem, hbm, vmem, hbm],
        out_specs=vmem,
        scratch_shapes=[pltpu.VMEM((LIVE, LIVE), BF)] * 3
        + [
            pltpu.VMEM((rows_v, LIVE), BF),
            pltpu.VMEM((columns, LIVE), BF),
            pltpu.SemaphoreType.DMA((2,)),
        ],
        compiler_params=pltpu.CompilerParams(vmem_limit_bytes=32 << 20),
        cost_estimate=pl.CostEstimate(flops=1 << 20, bytes_accessed=1 << 20, transcendentals=0),
        name="weight",
    )(core.reshape(1), piece, across, in_hbm(right), live, in_hbm(saved_sel))

    rows = left.shape[1]
    plan = (rows // 4, rows // 4, rows // 2)
    out = pl.pallas_call(
        functools.partial(product_kernel, plan),
        out_shape=jax.ShapeDtypeStruct((rows_v, rows), BF),
        in_specs=[vmem, hbm],
        out_specs=hbm,
        scratch_shapes=[
            pltpu.VMEM((nx, rows, width), BF),
            pltpu.VMEM((rows_v, rows), BF),
            pltpu.SemaphoreType.DMA((len(plan),)),
            pltpu.SemaphoreType.DMA((len(plan),)),
        ],
        compiler_params=pltpu.CompilerParams(vmem_limit_bytes=24 << 20),
        cost_estimate=pl.CostEstimate(flops=1 << 31, bytes_accessed=6 << 20, transcendentals=0),
        name="product",
    )(weight, in_hbm(left))
    return out.T


def solution(mesh):
    grid = Mesh(mesh.devices.reshape(4, 4, 8, 2), ("y", "x", "z", "c"))
    row = ("x", "z", "c")
    return jax.shard_map(
        on_device,
        mesh=grid,
        in_specs=(P(row, "y"), P(row, "y"), P(), P()),
        out_specs=P("y", row),
        check_vma=False,
    )
```

```python
import functools
import math

import jax
import jax.numpy as jnp
from jax import lax
from jax.experimental import pallas as pl
from jax.experimental.pallas import tpu as pltpu
from jax.sharding import Mesh, PartitionSpec as P

BF = jnp.bfloat16
F32 = jnp.float32
LIVE = 768
SIDE = 256
HALF = 128
Z = ("z4", "z2", "z1")
PAIRS = ((0, 0), (0, 1), (0, 2), (1, 1), (1, 2), (2, 2))


def select_matrix(ranks_ref, values_ref, sel, live_values, tasks, cap):
    row = lax.broadcasted_iota(jnp.int32, (cap, LIVE), 0)
    col = lax.broadcasted_iota(jnp.int32, (cap, LIVE), 1)
    diff = col - row
    offset = jnp.int32(0)
    upright = values_ref[...].T
    per_row = values_ref.shape[1] // cap
    picked = jnp.zeros((cap, LIVE), F32)
    for t in range(tasks):
        rank = ranks_ref[t]
        hit = (diff == offset) & (row < rank)
        sel[t * cap : (t + 1) * cap, :] = jnp.where(hit, 1.0, 0.0).astype(BF)
        at = t % per_row * cap
        column = upright[at : at + cap, t // per_row : t // per_row + 1]
        picked += jnp.where(hit, column, 0.0)
        offset = offset + rank
    live_values[...] = jnp.sum(picked, axis=0, keepdims=True)


def prepare_kernel(tasks, cap, u_ref, v_ref, ranks_ref, values_ref, stack_ref, sel_ref, live_ref, u_in, v_in, ranks, values, load):
    shards, rows_u = stack_ref.shape[0], u_ref.shape[0]
    loads = [
        pltpu.make_async_copy(src, dst, load.at[i])
        for i, (src, dst) in enumerate(((ranks_ref, ranks), (values_ref, values), (u_ref, u_in), (v_ref, v_in)))
    ]
    for copy in loads:
        copy.start()
    for copy in loads:
        copy.wait()
    for s in range(shards):
        stack_ref[s, :rows_u, :] = u_in[...]
        stack_ref[s, rows_u:, :] = v_in[...]
    select_matrix(ranks, values, sel_ref, live_ref, tasks, cap)


def gram_kernel(rows_u, place_ref, core_ref, x_ref, sel, keep_ref, give_ref, right_ref, sel_ref, right, left, sems):
    shards = x_ref.shape[0]
    save_sel = pltpu.make_async_copy(sel, sel_ref, sems.at[0])
    save_sel.start()
    width = x_ref.shape[2]
    place, core = place_ref[0], core_ref[0]
    total = None
    for s in range(shards):
        part = jnp.dot(x_ref[s, rows_u:, :], sel[s * width : (s + 1) * width, :], preferred_element_type=F32)
        total = part if total is None else total + part
    right[...] = total.astype(BF)
    save_right = pltpu.make_async_copy(right, right_ref, sems.at[1])
    save_right.start()

    @pl.when(place < 2)
    def _():
        total = None
        for s in range(shards):
            part = jnp.dot(x_ref[s, :rows_u, :], sel[s * width : (s + 1) * width, :], preferred_element_type=F32)
            total = part if total is None else total + part
        left[...] = total.astype(BF)

    for y in range(shards):

        @pl.when(place == y)
        def _():
            base = left if y < 2 else right
            for b in range(3):
                i, j = PAIRS[(y % 2) * 3 + b]
                block = lax.dot_general(
                    base[:, i * SIDE : (i + 1) * SIDE],
                    base[:, j * SIDE : (j + 1) * SIDE],
                    (((0,), (0,)), ((), ())),
                    preferred_element_type=F32,
                )
                for h in range(2):
                    c, k = divmod(b * 2 + h, 3)
                    half = block[:, h * HALF : (h + 1) * HALF]

                    @pl.when(core == c)
                    def _():
                        keep_ref[k * SIDE : (k + 1) * SIDE, :] = half

                    @pl.when(core != c)
                    def _():
                        give_ref[k * SIDE : (k + 1) * SIDE, :] = half.astype(BF)

    save_sel.wait()
    save_right.wait()


def load_gram(core, own_ref, other_ref, side, full):
    def blocks():
        for p, (i, j) in enumerate(PAIRS):
            y, b = side * 2 + p // 3, p % 3
            for h in range(2):
                c, k = divmod(b * 2 + h, 3)
                yield i, j, h, jnp.where(core == c, own_ref[y, k], other_ref[y, k]).astype(F32)

    squares = jnp.zeros((SIDE, HALF), F32)
    for i, j, _, block in blocks():
        squares += block * block * (1.0 if i == j else 2.0)
    norm = jnp.sqrt(jnp.sum(squares, keepdims=True))
    inverse = 1.0 / norm
    for i, j, h, block in blocks():
        scaled = (block * inverse).astype(BF)
        full[i * SIDE : (i + 1) * SIDE, j * SIDE + h * HALF : j * SIDE + (h + 1) * HALF] = scaled
        if i != j:
            full[j * SIDE + h * HALF : j * SIDE + (h + 1) * HALF, i * SIDE : (i + 1) * SIDE] = scaled.T
    return norm


def mm(a, b):
    return jnp.dot(a.astype(BF), b, preferred_element_type=F32)


def mirror(ref, i, block):
    rows = slice(i * SIDE, (i + 1) * SIDE)
    ref[rows, i * SIDE :] = block
    for j in range(i + 1, LIVE // SIDE):
        ref[j * SIDE : (j + 1) * SIDE, rows] = block[:, (j - i) * SIDE : (j - i + 1) * SIDE].T


def second_power(a0, a2):
    for i in range(LIVE // SIDE):
        mirror(a2, i, mm(a0[i * SIDE : (i + 1) * SIDE, :], a0[:, i * SIDE :]).astype(BF))


def next_inner(a0, a2, a1):
    for i in range(LIVE // SIDE):
        rows = slice(i * SIDE, (i + 1) * SIDE)
        cube = mm(a2[rows, :], a0[:, i * SIDE :])
        linear = 2.25 * a0[rows, i * SIDE :].astype(F32) - 1.5 * a2[rows, i * SIDE :].astype(F32)
        mirror(a1, i, (linear + 0.25 * cube).astype(BF))


def step(x, a):
    return 1.5 * x - 0.5 * mm(x, a[...])


def last_step(x, a1):
    return 1.5 * x - 0.5 * step(step(mm(x, a1[...]), a1), a1)


def finish_kernel(at_ref, own_ref, other_ref, right_ref, live_ref, sel_ref, *refs):
    parts, (out_ref, v0, v1, v2, u0, u1, u2, right, sel, weight, left, out, sems, left_sem, out_sem) = refs[:16], refs[16:]
    load_right = pltpu.make_async_copy(right_ref, right, sems.at[0])
    load_sel = pltpu.make_async_copy(sel_ref, sel, sems.at[1])
    load_right.start()
    load_sel.start()
    x_place, z, core = at_ref[0], at_ref[1], at_ref[2]
    shards, blocks, cores, rows, width = left.shape
    half = blocks // 2
    fetch = []
    for h in range(2):
        for n in range(cores):
            for m, step_x in enumerate((0, shards - 1, 1, 2)):
                dst = left.at[lax.rem(x_place + step_x, shards), pl.ds(h * half, half), (core, 1 - core)[n]]
                fetch.append(pltpu.make_async_copy(parts[n * 8 + h * 4 + m], dst, left_sem.at[h, n, m]))
    for copy in fetch:
        copy.start()

    norm_v = load_gram(core, own_ref, other_ref, 1, v0)
    second_power(v0, v2)
    norm_u = load_gram(core, own_ref, other_ref, 0, u0)
    load_right.wait()
    x = step(right[...].astype(F32), v0)
    next_inner(v0, v2, v1)
    second_power(u0, u2)
    x = step(x, v1)
    next_inner(u0, u2, u1)
    x = last_step(x, v1) * live_ref[...]
    x = last_step(step(step(x, u0), u1), u1)
    x = x * (lax.rsqrt(norm_v) * lax.rsqrt(norm_u))
    load_sel.wait()
    weight[...] = lax.dot_general(
        x.astype(BF), sel[...], (((1,), (1,)), ((), ())), preferred_element_type=F32
    ).astype(BF)

    for copy in fetch:
        copy.wait()
    tile = cores * rows
    store = []
    for at in range(0, blocks, half):
        for k in range(at, at + half, 2):
            total = None
            for s in range(shards):
                term = lax.dot_general(
                    weight[:, s * width : (s + 1) * width],
                    left[s, k : k + 2].reshape(2 * tile, width),
                    (((1,), (1,)), ((), ())),
                    preferred_element_type=F32,
                )
                total = term if total is None else total + term
            out[:, k * tile : (k + 2) * tile] = total.astype(BF)
        for k in range(at, at + half):
            bits = k % 2 * 4 + k // 2 % 2 * 2 + k // 4
            there = pl.ds(pl.multiple_of(jnp.bitwise_xor(z, bits) * tile, tile), tile)
            store.append(pltpu.make_async_copy(out.at[:, pl.ds(k * tile, tile)], out_ref.at[:, there], out_sem.at[k]))
            store[k].start()
    for copy in store:
        copy.wait()


def on_device(u_basis, v_basis, singular, ranks):
    tasks = ranks.shape[0]
    columns = singular.shape[0]
    cap = columns // tasks
    rows_u, width = u_basis.shape
    rows_v = v_basis.shape[0]
    ny, nx, nc = (lax.axis_size(a) for a in ("y", "x", "c"))
    nz = math.prod(lax.axis_size(a) for a in Z)
    place = lax.axis_index("y")
    core = lax.axis_index("c")
    vmem = pl.BlockSpec(memory_space=pltpu.VMEM)
    smem = pl.BlockSpec(memory_space=pltpu.SMEM)
    hbm = pl.BlockSpec(memory_space=pltpu.HBM)
    in_hbm = lambda a: pltpu.with_memory_space_constraint(a, pltpu.HBM)

    turned = []
    for k in range(2):
        swap = []
        for a in range(ny):
            for b in range(nx):
                swap += [((a * nx + b) * 2 + g, (b * nx + a) * 2 + (g ^ k)) for g in range(2)]
        turned.append(lax.ppermute(u_basis, ("y", "x", "z4"), swap))
    stack, sel, live = pl.pallas_call(
        functools.partial(prepare_kernel, tasks, cap),
        out_shape=(
            jax.ShapeDtypeStruct((ny, rows_u + rows_v, width), BF),
            jax.ShapeDtypeStruct((columns, LIVE), BF),
            jax.ShapeDtypeStruct((1, LIVE), F32),
        ),
        in_specs=[hbm] * 4,
        out_specs=(vmem, vmem, vmem),
        scratch_shapes=[
            pltpu.VMEM(u_basis.shape, BF),
            pltpu.VMEM(v_basis.shape, BF),
            pltpu.SMEM(ranks.shape, jnp.int32),
            pltpu.VMEM((columns // HALF, HALF), F32),
            pltpu.SemaphoreType.DMA((4,)),
        ],
        compiler_params=pltpu.CompilerParams(vmem_limit_bytes=16 << 20),
        name="prepare",
    )(in_hbm(u_basis), in_hbm(v_basis), in_hbm(ranks), in_hbm(singular.reshape(columns // HALF, HALF)))
    flip = [(0, 1), (1, 0)]
    near = jnp.stack(turned)
    near = jnp.concatenate([near, lax.ppermute(near, "z2", flip)])

    full = lax.all_to_all(stack, "y", 0, 0)
    full, near = lax.optimization_barrier((full, near))
    halves = [near, lax.ppermute(near, "z1", flip)]

    half = 3 * SIDE
    keep, give, right, saved_sel = pl.pallas_call(
        functools.partial(gram_kernel, rows_u),
        out_shape=(
            jax.ShapeDtypeStruct((half, HALF), F32),
            jax.ShapeDtypeStruct((half, HALF), BF),
            pltpu.HBM((rows_v, LIVE), BF),
            pltpu.HBM((columns, LIVE), BF),
        ),
        in_specs=[smem, smem, vmem, vmem],
        out_specs=(vmem, vmem, hbm, hbm),
        scratch_shapes=[
            pltpu.VMEM((rows_v, LIVE), BF),
            pltpu.VMEM((rows_u, LIVE), BF),
            pltpu.SemaphoreType.DMA((2,)),
        ],
        compiler_params=pltpu.CompilerParams(vmem_limit_bytes=24 << 20),
        cost_estimate=pl.CostEstimate(flops=1 << 30, bytes_accessed=4 << 20, transcendentals=0),
        name="gram",
    )(place.reshape(1), core.reshape(1), full, sel)

    mine = keep + lax.ppermute(give, "c", flip).astype(F32)
    spread = lax.all_to_all(mine.astype(BF).reshape(nx * nz, half // (nx * nz), HALF), ("x",) + Z, 0, 0)
    up = [(a, (a + 1) % nx) for a in range(nx)]
    down = [(b, a) for a, b in up]
    before = [lax.ppermute(h, "x", up) for h in halves]
    after = [lax.ppermute(h, "x", down) for h in halves]
    spread, before[0], after[0] = lax.optimization_barrier((spread, before[0], after[0]))
    piece = jnp.sum(spread.astype(F32), axis=0).astype(BF)

    piece = lax.all_to_all(jnp.broadcast_to(piece[None], (nz,) + piece.shape), Z, 0, 0)
    over = [(a, (a + 2) % nx) for a in range(nx)]
    across = [lax.ppermute(after[0], "x", down), lax.ppermute(halves[1], "x", over)]
    piece, before[1], after[1], across[0] = lax.optimization_barrier((piece, before[1], after[1], across[0]))
    parts = [p for h in range(2) for p in (halves[h], before[h], after[h], across[h])]
    parts += [lax.ppermute(p, "c", flip) for p in parts]
    piece = piece.reshape(-1, HALF)
    piece = lax.all_to_all(jnp.broadcast_to(piece[None], (ny * nx,) + piece.shape), ("y", "x"), 0, 0)
    piece, parts = lax.optimization_barrier((piece, parts))
    piece = piece.reshape(ny, 3, SIDE, HALF)
    other = lax.ppermute(piece, "c", flip)

    rows = nz * nc * rows_u
    here = jnp.stack([lax.axis_index("x"), lax.axis_index(Z), core])
    out = pl.pallas_call(
        finish_kernel,
        out_shape=jax.ShapeDtypeStruct((rows_v, rows), BF),
        in_specs=[smem, vmem, vmem, hbm, vmem, hbm] + [hbm] * len(parts),
        out_specs=hbm,
        scratch_shapes=[pltpu.VMEM((LIVE, LIVE), BF)] * 6
        + [
            pltpu.VMEM((rows_v, LIVE), BF),
            pltpu.VMEM((columns, LIVE), BF),
            pltpu.VMEM((rows_v, columns), BF),
            pltpu.VMEM((nx, nz, nc, rows_u, width), BF),
            pltpu.VMEM((rows_v, rows), BF),
            pltpu.SemaphoreType.DMA((2,)),
            pltpu.SemaphoreType.DMA((2, nc, 4)),
            pltpu.SemaphoreType.DMA((nz,)),
        ],
        compiler_params=pltpu.CompilerParams(vmem_limit_bytes=44 << 20),
        cost_estimate=pl.CostEstimate(flops=12 << 30, bytes_accessed=12 << 20, transcendentals=0),
        name="finish",
    )(here, piece, other, in_hbm(right), live, in_hbm(saved_sel), *[in_hbm(p) for p in parts])
    return out.T


def solution(mesh):
    grid = Mesh(mesh.devices.reshape(4, 4, 2, 2, 2, 2), ("y", "x") + Z + ("c",))
    row = ("x",) + Z + ("c",)
    return jax.shard_map(
        on_device,
        mesh=grid,
        in_specs=(P(row, "y"), P(row, "y"), P(), P()),
        out_specs=P("y", row),
        check_vma=False,
    )
```

```python
import functools
import math

import jax
import jax.numpy as jnp
from jax import lax
from jax.experimental import pallas as pl
from jax.experimental.pallas import tpu as pltpu
from jax.sharding import Mesh, PartitionSpec as P

BF = jnp.bfloat16
F32 = jnp.float32
LIVE = 768
SIDE = 256
HALF = 128
Z = ("z4", "z2", "z1")
PAIRS = ((0, 0), (0, 1), (0, 2), (1, 1), (1, 2), (2, 2))


def select_matrix(ranks_ref, values_ref, sel, live_values, tasks, cap):
    row = lax.broadcasted_iota(jnp.int32, (cap, LIVE), 0)
    col = lax.broadcasted_iota(jnp.int32, (cap, LIVE), 1)
    diff = col - row
    offset = jnp.int32(0)
    upright = values_ref[...].T
    per_row = values_ref.shape[1] // cap
    picked = jnp.zeros((cap, LIVE), F32)
    for t in range(tasks):
        rank = ranks_ref[t]
        hit = (diff == offset) & (row < rank)
        sel[t * cap : (t + 1) * cap, :] = jnp.where(hit, 1.0, 0.0).astype(BF)
        at = t % per_row * cap
        column = upright[at : at + cap, t // per_row : t // per_row + 1]
        picked += jnp.where(hit, column, 0.0)
        offset = offset + rank
    live_values[...] = jnp.sum(picked, axis=0, keepdims=True)


def prepare_kernel(tasks, cap, u_ref, v_ref, ranks_ref, values_ref, stack_ref, sel_ref, live_ref, u_in, v_in, ranks, values, load):
    shards, rows_u = stack_ref.shape[0], u_ref.shape[0]
    loads = [
        pltpu.make_async_copy(src, dst, load.at[i])
        for i, (src, dst) in enumerate(((ranks_ref, ranks), (values_ref, values), (u_ref, u_in), (v_ref, v_in)))
    ]
    for copy in loads:
        copy.start()
    for copy in loads:
        copy.wait()
    for s in range(shards):
        stack_ref[s, :rows_u, :] = u_in[...]
        stack_ref[s, rows_u:, :] = v_in[...]
    select_matrix(ranks, values, sel_ref, live_ref, tasks, cap)


def gram_kernel(rows_u, place_ref, core_ref, x_ref, sel, keep_ref, give_ref, right_ref, sel_ref, right, left, sems):
    shards = x_ref.shape[0]
    save_sel = pltpu.make_async_copy(sel, sel_ref, sems.at[0])
    save_sel.start()
    width = x_ref.shape[2]
    place, core = place_ref[0], core_ref[0]
    total = None
    for s in range(shards):
        part = jnp.dot(x_ref[s, rows_u:, :], sel[s * width : (s + 1) * width, :], preferred_element_type=F32)
        total = part if total is None else total + part
    right[...] = total.astype(BF)
    save_right = pltpu.make_async_copy(right, right_ref, sems.at[1])
    save_right.start()

    @pl.when(place < 2)
    def _():
        total = None
        for s in range(shards):
            part = jnp.dot(x_ref[s, :rows_u, :], sel[s * width : (s + 1) * width, :], preferred_element_type=F32)
            total = part if total is None else total + part
        left[...] = total.astype(BF)

    for y in range(shards):

        @pl.when(place == y)
        def _():
            base = left if y < 2 else right
            for b in range(3):
                i, j = PAIRS[(y % 2) * 3 + b]
                block = lax.dot_general(
                    base[:, i * SIDE : (i + 1) * SIDE],
                    base[:, j * SIDE : (j + 1) * SIDE],
                    (((0,), (0,)), ((), ())),
                    preferred_element_type=F32,
                )
                for h in range(2):
                    c, k = divmod(b * 2 + h, 3)
                    half = block[:, h * HALF : (h + 1) * HALF]

                    @pl.when(core == c)
                    def _():
                        keep_ref[k * SIDE : (k + 1) * SIDE, :] = half

                    @pl.when(core != c)
                    def _():
                        give_ref[k * SIDE : (k + 1) * SIDE, :] = half.astype(BF)

    save_sel.wait()
    save_right.wait()


def load_gram(core, own_ref, other_ref, side, full):
    square = jnp.zeros((1, 1), F32)
    blocks = []
    for p, (i, j) in enumerate(PAIRS):
        y, b = side * 2 + p // 3, p % 3
        for h in range(2):
            c, k = divmod(b * 2 + h, 3)
            block = jnp.where(core == c, own_ref[y, k].astype(F32), other_ref[y, k].astype(F32))
            square += jnp.sum(block * block, keepdims=True) * (1.0 if i == j else 2.0)
            blocks.append((i, j, h, block))
    norm = jnp.sqrt(square)
    inverse = 1.0 / norm
    for i, j, h, block in blocks:
        scaled = block * inverse
        full[i * SIDE : (i + 1) * SIDE, j * SIDE + h * HALF : j * SIDE + (h + 1) * HALF] = scaled.astype(BF)
        if i != j:
            full[j * SIDE + h * HALF : j * SIDE + (h + 1) * HALF, i * SIDE : (i + 1) * SIDE] = scaled.T.astype(BF)
    return norm


def mm(a, b):
    return jnp.dot(a.astype(BF), b, preferred_element_type=F32)


def mirror(ref, i, block):
    rows = slice(i * SIDE, (i + 1) * SIDE)
    ref[rows, i * SIDE :] = block
    for j in range(i + 1, LIVE // SIDE):
        ref[j * SIDE : (j + 1) * SIDE, rows] = block[:, (j - i) * SIDE : (j - i + 1) * SIDE].T


def second_power(a0, a2):
    for i in range(LIVE // SIDE):
        mirror(a2, i, mm(a0[i * SIDE : (i + 1) * SIDE, :], a0[:, i * SIDE :]).astype(BF))


def next_inner(a0, a2, a1):
    for i in range(LIVE // SIDE):
        rows = slice(i * SIDE, (i + 1) * SIDE)
        cube = mm(a2[rows, :], a0[:, i * SIDE :])
        linear = 2.25 * a0[rows, i * SIDE :].astype(F32) - 1.5 * a2[rows, i * SIDE :].astype(F32)
        mirror(a1, i, (linear + 0.25 * cube).astype(BF))


def step(x, a):
    return 1.5 * x - 0.5 * mm(x, a[...])


def last_step(x, a1):
    return 1.5 * x - 0.5 * step(step(mm(x, a1[...]), a1), a1)


def finish_kernel(at_ref, own_ref, other_ref, right_ref, live_ref, sel_ref, *refs):
    parts, (out_ref, v0, v1, v2, u0, u1, u2, right, sel, weight, left, out, sems, left_sem, out_sem) = refs[:14], refs[14:]
    load_right = pltpu.make_async_copy(right_ref, right, sems.at[0])
    load_sel = pltpu.make_async_copy(sel_ref, sel, sems.at[1])
    load_right.start()
    load_sel.start()
    x_place, z, core = at_ref[0], at_ref[1], at_ref[2]
    shards, blocks, cores, rows, width = left.shape
    half = blocks // 2
    fetch = []
    for h in range(2):
        for n in range(cores):
            span = pl.ds(h * half, half)
            sources = (parts[n * 7].at[span], *parts[n * 7 + 1 + h * 3 : n * 7 + 4 + h * 3])
            for m, (src, step_x) in enumerate(zip(sources, (0, shards - 1, 1, 2))):
                dst = left.at[lax.rem(x_place + step_x, shards), span, (core, 1 - core)[n]]
                fetch.append(pltpu.make_async_copy(src, dst, left_sem.at[h, n, m]))
    for copy in fetch:
        copy.start()

    norm_v = load_gram(core, own_ref, other_ref, 1, v0)
    second_power(v0, v2)
    load_right.wait()
    x = step(right[...].astype(F32), v0)
    norm_u = load_gram(core, own_ref, other_ref, 0, u0)
    next_inner(v0, v2, v1)
    second_power(u0, u2)
    x = step(x, v1)
    next_inner(u0, u2, u1)
    x = last_step(x, v1) * live_ref[...]
    x = last_step(step(step(x, u0), u1), u1)
    x = x * (lax.rsqrt(norm_v) * lax.rsqrt(norm_u))
    load_sel.wait()
    weight[...] = lax.dot_general(
        x.astype(BF), sel[...], (((1,), (1,)), ((), ())), preferred_element_type=F32
    ).astype(BF)

    for copy in fetch:
        copy.wait()
    tile = cores * rows
    store = []
    for at in range(0, blocks, half):
        for k in range(at, at + half, 2):
            total = None
            for s in range(shards):
                term = lax.dot_general(
                    weight[:, s * width : (s + 1) * width],
                    left[s, k : k + 2].reshape(2 * tile, width),
                    (((1,), (1,)), ((), ())),
                    preferred_element_type=F32,
                )
                total = term if total is None else total + term
            out[:, k * tile : (k + 2) * tile] = total.astype(BF)
        for k in range(at, at + half):
            bits = k % 2 * 4 + k // 2 % 2 * 2 + k // 4
            there = pl.ds(pl.multiple_of(jnp.bitwise_xor(z, bits) * tile, tile), tile)
            store.append(pltpu.make_async_copy(out.at[:, pl.ds(k * tile, tile)], out_ref.at[:, there], out_sem.at[k]))
            store[k].start()
    for copy in store:
        copy.wait()


def on_device(u_basis, v_basis, singular, ranks):
    tasks = ranks.shape[0]
    columns = singular.shape[0]
    cap = columns // tasks
    rows_u, width = u_basis.shape
    rows_v = v_basis.shape[0]
    ny, nx, nc = (lax.axis_size(a) for a in ("y", "x", "c"))
    nz = math.prod(lax.axis_size(a) for a in Z)
    place = lax.axis_index("y")
    core = lax.axis_index("c")
    vmem = pl.BlockSpec(memory_space=pltpu.VMEM)
    smem = pl.BlockSpec(memory_space=pltpu.SMEM)
    hbm = pl.BlockSpec(memory_space=pltpu.HBM)
    in_hbm = lambda a: pltpu.with_memory_space_constraint(a, pltpu.HBM)

    swap = [(a * nx + b, b * nx + a) for a in range(ny) for b in range(nx)]
    turned = lax.ppermute(u_basis, ("y", "x"), swap)
    stack, sel, live = pl.pallas_call(
        functools.partial(prepare_kernel, tasks, cap),
        out_shape=(
            jax.ShapeDtypeStruct((ny, rows_u + rows_v, width), BF),
            jax.ShapeDtypeStruct((columns, LIVE), BF),
            jax.ShapeDtypeStruct((1, LIVE), F32),
        ),
        in_specs=[hbm] * 4,
        out_specs=(vmem, vmem, vmem),
        scratch_shapes=[
            pltpu.VMEM(u_basis.shape, BF),
            pltpu.VMEM(v_basis.shape, BF),
            pltpu.SMEM(ranks.shape, jnp.int32),
            pltpu.VMEM((columns // HALF, HALF), F32),
            pltpu.SemaphoreType.DMA((4,)),
        ],
        compiler_params=pltpu.CompilerParams(vmem_limit_bytes=16 << 20),
        name="prepare",
    )(in_hbm(u_basis), in_hbm(v_basis), in_hbm(ranks), in_hbm(singular.reshape(columns // HALF, HALF)))
    flip = [(0, 1), (1, 0)]
    turned, stack, sel, live = lax.optimization_barrier((turned, stack, sel, live))
    near = jnp.stack([turned, lax.ppermute(turned, "z4", flip)])
    near = jnp.concatenate([near, lax.ppermute(near, "z2", flip)])

    full = lax.all_to_all(stack, "y", 0, 0)
    full, near = lax.optimization_barrier((full, near))
    halves = [near, lax.ppermute(near, "z1", flip)]

    half = 3 * SIDE
    keep, give, right, saved_sel = pl.pallas_call(
        functools.partial(gram_kernel, rows_u),
        out_shape=(
            jax.ShapeDtypeStruct((half, HALF), F32),
            jax.ShapeDtypeStruct((half, HALF), BF),
            pltpu.HBM((rows_v, LIVE), BF),
            pltpu.HBM((columns, LIVE), BF),
        ),
        in_specs=[smem, smem, vmem, vmem],
        out_specs=(vmem, vmem, hbm, hbm),
        scratch_shapes=[
            pltpu.VMEM((rows_v, LIVE), BF),
            pltpu.VMEM((rows_u, LIVE), BF),
            pltpu.SemaphoreType.DMA((2,)),
        ],
        compiler_params=pltpu.CompilerParams(vmem_limit_bytes=24 << 20),
        cost_estimate=pl.CostEstimate(flops=1 << 30, bytes_accessed=4 << 20, transcendentals=0),
        name="gram",
    )(place.reshape(1), core.reshape(1), full, sel)

    mine = keep + lax.ppermute(give, "c", flip).astype(F32)
    spread = lax.all_to_all(mine.astype(BF).reshape(nx * nz, half // (nx * nz), HALF), ("x",) + Z, 0, 0)
    up = [(a, (a + 1) % nx) for a in range(nx)]
    down = [(b, a) for a, b in up]
    before = [lax.ppermute(h, "x", up) for h in halves]
    after = [lax.ppermute(h, "x", down) for h in halves]
    own = jnp.concatenate(halves)
    spread, own = lax.optimization_barrier((spread, own))
    piece = jnp.sum(spread.astype(F32), axis=0).astype(BF)

    piece = lax.all_to_all(jnp.broadcast_to(piece[None], (nz,) + piece.shape), Z, 0, 0)
    over = [(a, (a + 2) % nx) for a in range(nx)]
    across = [lax.ppermute(after[0], "x", down), lax.ppermute(halves[1], "x", over)]
    piece, before, after = lax.optimization_barrier((piece, before, after))
    parts = [own] + [p for h in range(2) for p in (before[h], after[h], across[h])]
    parts += [lax.ppermute(p, "c", flip) for p in parts]
    piece = piece.reshape(-1, HALF)
    piece = lax.all_to_all(jnp.broadcast_to(piece[None], (ny * nx,) + piece.shape), ("y", "x"), 0, 0)
    piece, parts = lax.optimization_barrier((piece, parts))
    piece = piece.reshape(ny, 3, SIDE, HALF)
    other = lax.ppermute(piece, "c", flip)

    rows = nz * nc * rows_u
    here = jnp.stack([lax.axis_index("x"), lax.axis_index(Z), core])
    out = pl.pallas_call(
        finish_kernel,
        out_shape=jax.ShapeDtypeStruct((rows_v, rows), BF),
        in_specs=[smem, vmem, vmem, hbm, vmem, hbm] + [hbm] * len(parts),
        out_specs=hbm,
        scratch_shapes=[pltpu.VMEM((LIVE, LIVE), BF)] * 6
        + [
            pltpu.VMEM((rows_v, LIVE), BF),
            pltpu.VMEM((columns, LIVE), BF),
            pltpu.VMEM((rows_v, columns), BF),
            pltpu.VMEM((nx, nz, nc, rows_u, width), BF),
            pltpu.VMEM((rows_v, rows), BF),
            pltpu.SemaphoreType.DMA((2,)),
            pltpu.SemaphoreType.DMA((2, nc, 4)),
            pltpu.SemaphoreType.DMA((nz,)),
        ],
        compiler_params=pltpu.CompilerParams(vmem_limit_bytes=44 << 20),
        cost_estimate=pl.CostEstimate(flops=12 << 30, bytes_accessed=12 << 20, transcendentals=0),
        name="finish",
    )(here, piece, other, in_hbm(right), live, in_hbm(saved_sel), *[in_hbm(p) for p in parts])
    return out.T


def solution(mesh):
    grid = Mesh(mesh.devices.reshape(4, 4, 2, 2, 2, 2), ("y", "x") + Z + ("c",))
    row = ("x",) + Z + ("c",)
    return jax.shard_map(
        on_device,
        mesh=grid,
        in_specs=(P(row, "y"), P(row, "y"), P(), P()),
        out_specs=P("y", row),
        check_vma=False,
    )
```

```python
import functools
import math

import jax
import jax.numpy as jnp
from jax import lax
from jax.experimental import pallas as pl
from jax.experimental.pallas import tpu as pltpu
from jax.sharding import Mesh, PartitionSpec as P

BF = jnp.bfloat16
F32 = jnp.float32
LIVE = 768
SIDE = 256
HALF = 128
Z = ("z4", "z2", "z1")
PAIRS = ((0, 0), (0, 1), (0, 2), (1, 1), (1, 2), (2, 2))


def select_matrix(ranks_ref, values_ref, sel, live_values, tasks, cap):
    row = lax.broadcasted_iota(jnp.int32, (cap, LIVE), 0)
    col = lax.broadcasted_iota(jnp.int32, (cap, LIVE), 1)
    diff = col - row
    offset = jnp.int32(0)
    upright = values_ref[...].T
    per_row = values_ref.shape[1] // cap
    picked = jnp.zeros((cap, LIVE), F32)
    for t in range(tasks):
        rank = ranks_ref[t]
        hit = (diff == offset) & (row < rank)
        sel[t * cap : (t + 1) * cap, :] = jnp.where(hit, 1.0, 0.0).astype(BF)
        at = t % per_row * cap
        column = upright[at : at + cap, t // per_row : t // per_row + 1]
        picked += jnp.where(hit, column, 0.0)
        offset = offset + rank
    live_values[...] = jnp.sum(picked, axis=0, keepdims=True)


def prepare_kernel(tasks, cap, u_ref, v_ref, ranks_ref, values_ref, stack_ref, sel_ref, live_ref, u_in, v_in, ranks, values, load):
    shards, rows_u = stack_ref.shape[0], u_ref.shape[0]
    loads = [
        pltpu.make_async_copy(src, dst, load.at[i])
        for i, (src, dst) in enumerate(((ranks_ref, ranks), (values_ref, values), (u_ref, u_in), (v_ref, v_in)))
    ]
    for copy in loads:
        copy.start()
    for copy in loads:
        copy.wait()
    for s in range(shards):
        stack_ref[s, :rows_u, :] = u_in[...]
        stack_ref[s, rows_u:, :] = v_in[...]
    select_matrix(ranks, values, sel_ref, live_ref, tasks, cap)


def gram_kernel(rows_u, place_ref, core_ref, x_ref, sel, keep_ref, give_ref, right_ref, sel_ref, right, left, sems):
    shards = x_ref.shape[0]
    save_sel = pltpu.make_async_copy(sel, sel_ref, sems.at[0])
    save_sel.start()
    width = x_ref.shape[2]
    place, core = place_ref[0], core_ref[0]
    total = None
    for s in range(shards):
        part = jnp.dot(x_ref[s, rows_u:, :], sel[s * width : (s + 1) * width, :], preferred_element_type=F32)
        total = part if total is None else total + part
    right[...] = total.astype(BF)
    save_right = pltpu.make_async_copy(right, right_ref, sems.at[1])
    save_right.start()

    @pl.when(place < 2)
    def _():
        total = None
        for s in range(shards):
            part = jnp.dot(x_ref[s, :rows_u, :], sel[s * width : (s + 1) * width, :], preferred_element_type=F32)
            total = part if total is None else total + part
        left[...] = total.astype(BF)

    for y in range(shards):

        @pl.when(place == y)
        def _():
            base = left if y < 2 else right
            for b in range(3):
                i, j = PAIRS[(y % 2) * 3 + b]
                block = lax.dot_general(
                    base[:, i * SIDE : (i + 1) * SIDE],
                    base[:, j * SIDE : (j + 1) * SIDE],
                    (((0,), (0,)), ((), ())),
                    preferred_element_type=F32,
                )
                for h in range(2):
                    c, k = divmod(b * 2 + h, 3)
                    half = block[:, h * HALF : (h + 1) * HALF]

                    @pl.when(core == c)
                    def _():
                        keep_ref[k * SIDE : (k + 1) * SIDE, :] = half

                    @pl.when(core != c)
                    def _():
                        give_ref[k * SIDE : (k + 1) * SIDE, :] = half.astype(BF)

    save_sel.wait()
    save_right.wait()


def load_gram(core, own_ref, other_ref, side, full):
    square = jnp.zeros((1, 1), F32)
    blocks = []
    for p, (i, j) in enumerate(PAIRS):
        y, b = side * 2 + p // 3, p % 3
        for h in range(2):
            c, k = divmod(b * 2 + h, 3)
            block = jnp.where(core == c, own_ref[y, k].astype(F32), other_ref[y, k].astype(F32))
            square += jnp.sum(block * block, keepdims=True) * (1.0 if i == j else 2.0)
            blocks.append((i, j, h, block))
    norm = jnp.sqrt(square)
    inverse = 1.0 / norm
    for i, j, h, block in blocks:
        scaled = block * inverse
        full[i * SIDE : (i + 1) * SIDE, j * SIDE + h * HALF : j * SIDE + (h + 1) * HALF] = scaled.astype(BF)
        if i != j:
            full[j * SIDE + h * HALF : j * SIDE + (h + 1) * HALF, i * SIDE : (i + 1) * SIDE] = scaled.T.astype(BF)
    return norm


def mm(a, b):
    return jnp.dot(a.astype(BF), b, preferred_element_type=F32)


def mirror(ref, i, block):
    rows = slice(i * SIDE, (i + 1) * SIDE)
    ref[rows, i * SIDE :] = block
    for j in range(i + 1, LIVE // SIDE):
        ref[j * SIDE : (j + 1) * SIDE, rows] = block[:, (j - i) * SIDE : (j - i + 1) * SIDE].T


def second_power(a0, a2):
    for i in range(LIVE // SIDE):
        mirror(a2, i, mm(a0[i * SIDE : (i + 1) * SIDE, :], a0[:, i * SIDE :]).astype(BF))


def next_inner(a0, a2, a1):
    for i in range(LIVE // SIDE):
        rows = slice(i * SIDE, (i + 1) * SIDE)
        cube = mm(a2[rows, :], a0[:, i * SIDE :])
        linear = 2.25 * a0[rows, i * SIDE :].astype(F32) - 1.5 * a2[rows, i * SIDE :].astype(F32)
        mirror(a1, i, (linear + 0.25 * cube).astype(BF))


def step(x, a):
    return 1.5 * x - 0.5 * mm(x, a[...])


def last_step(x, a1):
    return 1.5 * x - 0.5 * step(step(mm(x, a1[...]), a1), a1)


def finish_kernel(at_ref, own_ref, other_ref, right_ref, live_ref, sel_ref, *refs):
    parts, (out_ref, v0, v1, v2, u0, u1, u2, right, sel, weight, left, out, sems, left_sem, out_sem) = refs[:14], refs[14:]
    load_right = pltpu.make_async_copy(right_ref, right, sems.at[0])
    load_sel = pltpu.make_async_copy(sel_ref, sel, sems.at[1])
    load_right.start()
    load_sel.start()
    x_place, z, core = at_ref[0], at_ref[1], at_ref[2]
    shards, blocks, cores, rows, width = left.shape
    half = blocks // 2
    fetch = []
    for h in range(2):
        for n in range(cores):
            span = pl.ds(h * half, half)
            sources = (parts[n * 7].at[span], *parts[n * 7 + 1 + h * 3 : n * 7 + 4 + h * 3])
            for m, (src, step_x) in enumerate(zip(sources, (0, shards - 1, 1, 2))):
                dst = left.at[lax.rem(x_place + step_x, shards), span, (core, 1 - core)[n]]
                fetch.append(pltpu.make_async_copy(src, dst, left_sem.at[h, n, m]))

    norm_v = load_gram(core, own_ref, other_ref, 1, v0)
    second_power(v0, v2)
    load_right.wait()
    x = step(right[...].astype(F32), v0)
    norm_u = load_gram(core, own_ref, other_ref, 0, u0)
    for copy in fetch:
        copy.start()
    next_inner(v0, v2, v1)
    second_power(u0, u2)
    x = step(x, v1)
    next_inner(u0, u2, u1)
    x = last_step(x, v1) * live_ref[...]
    x = last_step(step(step(x, u0), u1), u1)
    x = x * (lax.rsqrt(norm_v) * lax.rsqrt(norm_u))
    load_sel.wait()
    high = x.astype(BF)
    pair = jnp.concatenate([high, (x - high.astype(F32)).astype(BF)])
    weight[...] = lax.dot_general(
        pair, sel[...], (((1,), (1,)), ((), ())), preferred_element_type=F32
    ).astype(BF)

    for copy in fetch:
        copy.wait()
    tile = cores * rows
    store = []
    for at in range(0, blocks, half):
        for k in range(at, at + half, 2):
            total = None
            for s in range(shards):
                term = lax.dot_general(
                    weight[:, s * width : (s + 1) * width],
                    left[s, k : k + 2].reshape(2 * tile, width),
                    (((1,), (1,)), ((), ())),
                    preferred_element_type=F32,
                )
                total = term if total is None else total + term
            rows_v = out.shape[0]
            out[:, k * tile : (k + 2) * tile] = (total[:rows_v] + total[rows_v:]).astype(BF)
        for k in range(at, at + half):
            bits = k % 2 * 4 + k // 2 % 2 * 2 + k // 4
            there = pl.ds(pl.multiple_of(jnp.bitwise_xor(z, bits) * tile, tile), tile)
            store.append(pltpu.make_async_copy(out.at[:, pl.ds(k * tile, tile)], out_ref.at[:, there], out_sem.at[k]))
            store[k].start()
    for copy in store:
        copy.wait()


def on_device(u_basis, v_basis, singular, ranks):
    tasks = ranks.shape[0]
    columns = singular.shape[0]
    cap = columns // tasks
    rows_u, width = u_basis.shape
    rows_v = v_basis.shape[0]
    ny, nx, nc = (lax.axis_size(a) for a in ("y", "x", "c"))
    nz = math.prod(lax.axis_size(a) for a in Z)
    place = lax.axis_index("y")
    core = lax.axis_index("c")
    vmem = pl.BlockSpec(memory_space=pltpu.VMEM)
    smem = pl.BlockSpec(memory_space=pltpu.SMEM)
    hbm = pl.BlockSpec(memory_space=pltpu.HBM)
    in_hbm = lambda a: pltpu.with_memory_space_constraint(a, pltpu.HBM)

    swap = [(a * nx + b, b * nx + a) for a in range(ny) for b in range(nx)]
    turned = lax.ppermute(u_basis, ("y", "x"), swap)
    stack, sel, live = pl.pallas_call(
        functools.partial(prepare_kernel, tasks, cap),
        out_shape=(
            jax.ShapeDtypeStruct((ny, rows_u + rows_v, width), BF),
            jax.ShapeDtypeStruct((columns, LIVE), BF),
            jax.ShapeDtypeStruct((1, LIVE), F32),
        ),
        in_specs=[hbm] * 4,
        out_specs=(vmem, vmem, vmem),
        scratch_shapes=[
            pltpu.VMEM(u_basis.shape, BF),
            pltpu.VMEM(v_basis.shape, BF),
            pltpu.SMEM(ranks.shape, jnp.int32),
            pltpu.VMEM((columns // HALF, HALF), F32),
            pltpu.SemaphoreType.DMA((4,)),
        ],
        compiler_params=pltpu.CompilerParams(vmem_limit_bytes=16 << 20),
        name="prepare",
    )(in_hbm(u_basis), in_hbm(v_basis), in_hbm(ranks), in_hbm(singular.reshape(columns // HALF, HALF)))
    flip = [(0, 1), (1, 0)]
    turned, stack, sel, live = lax.optimization_barrier((turned, stack, sel, live))
    near = jnp.stack([turned, lax.ppermute(turned, "z4", flip)])
    near = jnp.concatenate([near, lax.ppermute(near, "z2", flip)])

    full = lax.all_to_all(stack, "y", 0, 0)
    full, near = lax.optimization_barrier((full, near))
    halves = [near, lax.ppermute(near, "z1", flip)]

    half = 3 * SIDE
    keep, give, right, saved_sel = pl.pallas_call(
        functools.partial(gram_kernel, rows_u),
        out_shape=(
            jax.ShapeDtypeStruct((half, HALF), F32),
            jax.ShapeDtypeStruct((half, HALF), BF),
            pltpu.HBM((rows_v, LIVE), BF),
            pltpu.HBM((columns, LIVE), BF),
        ),
        in_specs=[smem, smem, vmem, vmem],
        out_specs=(vmem, vmem, hbm, hbm),
        scratch_shapes=[
            pltpu.VMEM((rows_v, LIVE), BF),
            pltpu.VMEM((rows_u, LIVE), BF),
            pltpu.SemaphoreType.DMA((2,)),
        ],
        compiler_params=pltpu.CompilerParams(vmem_limit_bytes=24 << 20),
        cost_estimate=pl.CostEstimate(flops=1 << 30, bytes_accessed=4 << 20, transcendentals=0),
        name="gram",
    )(place.reshape(1), core.reshape(1), full, sel)

    mine = keep + lax.ppermute(give, "c", flip).astype(F32)
    spread = lax.all_to_all(mine.astype(BF).reshape(nx * nz, half // (nx * nz), HALF), ("x",) + Z, 0, 0)
    up = [(a, (a + 1) % nx) for a in range(nx)]
    down = [(b, a) for a, b in up]
    before = [lax.ppermute(h, "x", up) for h in halves]
    after = [lax.ppermute(h, "x", down) for h in halves]
    own = jnp.concatenate(halves)
    spread, own = lax.optimization_barrier((spread, own))
    piece = jnp.sum(spread.astype(F32), axis=0).astype(BF)

    piece = lax.all_to_all(jnp.broadcast_to(piece[None], (nz,) + piece.shape), Z, 0, 0)
    over = [(a, (a + 2) % nx) for a in range(nx)]
    across = [lax.ppermute(after[0], "x", down), lax.ppermute(halves[1], "x", over)]
    piece, before, after = lax.optimization_barrier((piece, before, after))
    parts = [own] + [p for h in range(2) for p in (before[h], after[h], across[h])]
    parts += [lax.ppermute(p, "c", flip) for p in parts]
    piece = piece.reshape(-1, HALF)
    piece = lax.all_to_all(jnp.broadcast_to(piece[None], (ny * nx,) + piece.shape), ("y", "x"), 0, 0)
    piece, parts = lax.optimization_barrier((piece, parts))
    piece = piece.reshape(ny, 3, SIDE, HALF)
    other = lax.ppermute(piece, "c", flip)

    rows = nz * nc * rows_u
    here = jnp.stack([lax.axis_index("x"), lax.axis_index(Z), core])
    out = pl.pallas_call(
        finish_kernel,
        out_shape=jax.ShapeDtypeStruct((rows_v, rows), BF),
        in_specs=[smem, vmem, vmem, hbm, vmem, hbm] + [hbm] * len(parts),
        out_specs=hbm,
        scratch_shapes=[pltpu.VMEM((LIVE, LIVE), BF)] * 6
        + [
            pltpu.VMEM((rows_v, LIVE), BF),
            pltpu.VMEM((columns, LIVE), BF),
            pltpu.VMEM((2 * rows_v, columns), BF),
            pltpu.VMEM((nx, nz, nc, rows_u, width), BF),
            pltpu.VMEM((rows_v, rows), BF),
            pltpu.SemaphoreType.DMA((2,)),
            pltpu.SemaphoreType.DMA((2, nc, 4)),
            pltpu.SemaphoreType.DMA((nz,)),
        ],
        compiler_params=pltpu.CompilerParams(vmem_limit_bytes=44 << 20),
        cost_estimate=pl.CostEstimate(flops=12 << 30, bytes_accessed=12 << 20, transcendentals=0),
        name="finish",
    )(here, piece, other, in_hbm(right), live, in_hbm(saved_sel), *[in_hbm(p) for p in parts])
    return out.T


def solution(mesh):
    grid = Mesh(mesh.devices.reshape(4, 4, 2, 2, 2, 2), ("y", "x") + Z + ("c",))
    row = ("x",) + Z + ("c",)
    return jax.shard_map(
        on_device,
        mesh=grid,
        in_specs=(P(row, "y"), P(row, "y"), P(), P()),
        out_specs=P("y", row),
        check_vma=False,
    )
```

```python
import functools
import math

import jax
import jax.numpy as jnp
from jax import lax
from jax.experimental import pallas as pl
from jax.experimental.pallas import tpu as pltpu
from jax.sharding import Mesh, PartitionSpec as P

BF = jnp.bfloat16
F32 = jnp.float32
LIVE = 768
SIDE = 256
HALF = 128
Z = ("z4", "z2", "z1")
PAIRS = ((0, 0), (0, 1), (0, 2), (1, 1), (1, 2), (2, 2))


def select_matrix(ranks_ref, values_ref, sel, live_values, tasks, cap):
    row = lax.broadcasted_iota(jnp.int32, (cap, LIVE), 0)
    col = lax.broadcasted_iota(jnp.int32, (cap, LIVE), 1)
    diff = col - row
    offset = jnp.int32(0)
    upright = values_ref[...].T
    per_row = values_ref.shape[1] // cap
    picked = jnp.zeros((cap, LIVE), F32)
    for t in range(tasks):
        rank = ranks_ref[t]
        hit = (diff == offset) & (row < rank)
        sel[t * cap : (t + 1) * cap, :] = jnp.where(hit, 1.0, 0.0).astype(BF)
        at = t % per_row * cap
        column = upright[at : at + cap, t // per_row : t // per_row + 1]
        picked += jnp.where(hit, column, 0.0)
        offset = offset + rank
    live_values[...] = jnp.sum(picked, axis=0, keepdims=True)


def prepare_kernel(tasks, cap, u_ref, v_ref, ranks_ref, values_ref, stack_ref, sel_ref, live_ref, u_in, v_in, ranks, values, load):
    shards, rows_u = stack_ref.shape[0], u_ref.shape[0]
    loads = [
        pltpu.make_async_copy(src, dst, load.at[i])
        for i, (src, dst) in enumerate(((ranks_ref, ranks), (values_ref, values), (u_ref, u_in), (v_ref, v_in)))
    ]
    for copy in loads:
        copy.start()
    for copy in loads:
        copy.wait()
    for s in range(shards):
        stack_ref[s, :rows_u, :] = u_in[...]
        stack_ref[s, rows_u:, :] = v_in[...]
    select_matrix(ranks, values, sel_ref, live_ref, tasks, cap)


def gram_kernel(rows_u, place_ref, core_ref, x_ref, sel, keep_ref, give_ref, right_ref, sel_ref, right, left, sems):
    shards = x_ref.shape[0]
    save_sel = pltpu.make_async_copy(sel, sel_ref, sems.at[0])
    save_sel.start()
    width = x_ref.shape[2]
    place, core = place_ref[0], core_ref[0]
    total = None
    for s in range(shards):
        part = jnp.dot(x_ref[s, rows_u:, :], sel[s * width : (s + 1) * width, :], preferred_element_type=F32)
        total = part if total is None else total + part
    right[...] = total.astype(BF)
    save_right = pltpu.make_async_copy(right, right_ref, sems.at[1])
    save_right.start()

    @pl.when(place < 2)
    def _():
        total = None
        for s in range(shards):
            part = jnp.dot(x_ref[s, :rows_u, :], sel[s * width : (s + 1) * width, :], preferred_element_type=F32)
            total = part if total is None else total + part
        left[...] = total.astype(BF)

    for y in range(shards):

        @pl.when(place == y)
        def _():
            base = left if y < 2 else right
            for b in range(3):
                i, j = PAIRS[(y % 2) * 3 + b]
                block = lax.dot_general(
                    base[:, i * SIDE : (i + 1) * SIDE],
                    base[:, j * SIDE : (j + 1) * SIDE],
                    (((0,), (0,)), ((), ())),
                    preferred_element_type=F32,
                )
                for h in range(2):
                    c, k = divmod(b * 2 + h, 3)
                    half = block[:, h * HALF : (h + 1) * HALF]

                    @pl.when(core == c)
                    def _():
                        keep_ref[k * SIDE : (k + 1) * SIDE, :] = half

                    @pl.when(core != c)
                    def _():
                        give_ref[k * SIDE : (k + 1) * SIDE, :] = half.astype(BF)

    save_sel.wait()
    save_right.wait()


def load_gram(core, own_ref, other_ref, side, full):
    square = jnp.zeros((1, 1), F32)
    blocks = []
    for p, (i, j) in enumerate(PAIRS):
        y, b = side * 2 + p // 3, p % 3
        for h in range(2):
            c, k = divmod(b * 2 + h, 3)
            block = jnp.where(core == c, own_ref[y, k].astype(F32), other_ref[y, k].astype(F32))
            square += jnp.sum(block * block, keepdims=True) * (1.0 if i == j else 2.0)
            blocks.append((i, j, h, block))
    norm = jnp.sqrt(square)
    inverse = 0.5 / norm
    for i, j, h, block in blocks:
        scaled = block * inverse
        full[i * SIDE : (i + 1) * SIDE, j * SIDE + h * HALF : j * SIDE + (h + 1) * HALF] = scaled.astype(BF)
        if i != j:
            full[j * SIDE + h * HALF : j * SIDE + (h + 1) * HALF, i * SIDE : (i + 1) * SIDE] = scaled.T.astype(BF)
    return norm


def mm(a, b):
    return jnp.dot(a.astype(BF), b, preferred_element_type=F32)


def mirror(ref, i, block):
    rows = slice(i * SIDE, (i + 1) * SIDE)
    ref[rows, i * SIDE :] = block
    for j in range(i + 1, LIVE // SIDE):
        ref[j * SIDE : (j + 1) * SIDE, rows] = block[:, (j - i) * SIDE : (j - i + 1) * SIDE].T


def second_power(a0, a2):
    for i in range(LIVE // SIDE):
        mirror(a2, i, mm(a0[i * SIDE : (i + 1) * SIDE, :], a0[:, i * SIDE :]).astype(BF))


def next_inner(a0, a2, a1):
    for i in range(LIVE // SIDE):
        rows = slice(i * SIDE, (i + 1) * SIDE)
        cube = mm(a2[rows, :], a0[:, i * SIDE :])
        linear = 2.25 * a0[rows, i * SIDE :].astype(F32) - 3.0 * a2[rows, i * SIDE :].astype(F32)
        mirror(a1, i, (linear + cube).astype(BF))


def step(x, a):
    return 1.5 * x - mm(x, a[...])


def last_step(x, a1):
    return 1.5 * x - step(step(mm(x, a1[...]), a1), a1)


def finish_kernel(at_ref, own_ref, other_ref, right_ref, live_ref, sel_ref, *refs):
    parts, (out_ref, v0, v1, v2, u0, u1, u2, right, sel, weight, left, out, sems, left_sem, out_sem) = refs[:14], refs[14:]
    load_right = pltpu.make_async_copy(right_ref, right, sems.at[0])
    load_sel = pltpu.make_async_copy(sel_ref, sel, sems.at[1])
    load_right.start()
    x_place, z, core = at_ref[0], at_ref[1], at_ref[2]
    shards, blocks, cores, rows, width = left.shape
    half = blocks // 2
    fetch = []
    for h in range(2):
        for n in range(cores):
            span = pl.ds(h * half, half)
            sources = (parts[n * 7].at[span], *parts[n * 7 + 1 + h * 3 : n * 7 + 4 + h * 3])
            for m, (src, step_x) in enumerate(zip(sources, (0, shards - 1, 1, 2))):
                dst = left.at[lax.rem(x_place + step_x, shards), span, (core, 1 - core)[n]]
                fetch.append(pltpu.make_async_copy(src, dst, left_sem.at[h, n, m]))

    norm_v = load_gram(core, own_ref, other_ref, 1, v0)
    second_power(v0, v2)
    load_right.wait()
    x = step(right[...].astype(F32), v0)
    norm_u = load_gram(core, own_ref, other_ref, 0, u0)
    load_sel.start()
    for copy in fetch:
        copy.start()
    next_inner(v0, v2, v1)
    second_power(u0, u2)
    x = step(x, v1)
    next_inner(u0, u2, u1)
    x = last_step(x, v1) * live_ref[...]
    x = last_step(step(step(x, u0), u1), u1)
    x = x * (lax.rsqrt(norm_v) * lax.rsqrt(norm_u))
    load_sel.wait()
    high = x.astype(BF)
    pair = jnp.concatenate([high, (x - high.astype(F32)).astype(BF)])
    weight[...] = lax.dot_general(
        pair, sel[...], (((1,), (1,)), ((), ())), preferred_element_type=F32
    ).astype(BF)

    for copy in fetch:
        copy.wait()
    tile = cores * rows
    store = []
    for at in range(0, blocks, half):
        for k in range(at, at + half, 2):
            total = None
            for s in range(shards):
                term = lax.dot_general(
                    weight[:, s * width : (s + 1) * width],
                    left[s, k : k + 2].reshape(2 * tile, width),
                    (((1,), (1,)), ((), ())),
                    preferred_element_type=F32,
                )
                total = term if total is None else total + term
            rows_v = out.shape[0]
            out[:, k * tile : (k + 2) * tile] = (total[:rows_v] + total[rows_v:]).astype(BF)
        for k in range(at, at + half):
            bits = k % 2 * 4 + k // 2 % 2 * 2 + k // 4
            there = pl.ds(pl.multiple_of(jnp.bitwise_xor(z, bits) * tile, tile), tile)
            store.append(pltpu.make_async_copy(out.at[:, pl.ds(k * tile, tile)], out_ref.at[:, there], out_sem.at[k]))
            store[k].start()
    for copy in store:
        copy.wait()


def on_device(u_basis, v_basis, singular, ranks):
    tasks = ranks.shape[0]
    columns = singular.shape[0]
    cap = columns // tasks
    rows_u, width = u_basis.shape
    rows_v = v_basis.shape[0]
    ny, nx, nc = (lax.axis_size(a) for a in ("y", "x", "c"))
    nz = math.prod(lax.axis_size(a) for a in Z)
    place = lax.axis_index("y")
    core = lax.axis_index("c")
    vmem = pl.BlockSpec(memory_space=pltpu.VMEM)
    smem = pl.BlockSpec(memory_space=pltpu.SMEM)
    hbm = pl.BlockSpec(memory_space=pltpu.HBM)
    in_hbm = lambda a: pltpu.with_memory_space_constraint(a, pltpu.HBM)

    swap = [(a * nx + b, b * nx + a) for a in range(ny) for b in range(nx)]
    turned = lax.ppermute(u_basis, ("y", "x"), swap)
    stack, sel, live = pl.pallas_call(
        functools.partial(prepare_kernel, tasks, cap),
        out_shape=(
            jax.ShapeDtypeStruct((ny, rows_u + rows_v, width), BF),
            jax.ShapeDtypeStruct((columns, LIVE), BF),
            jax.ShapeDtypeStruct((1, LIVE), F32),
        ),
        in_specs=[hbm] * 4,
        out_specs=(vmem, vmem, vmem),
        scratch_shapes=[
            pltpu.VMEM(u_basis.shape, BF),
            pltpu.VMEM(v_basis.shape, BF),
            pltpu.SMEM(ranks.shape, jnp.int32),
            pltpu.VMEM((columns // HALF, HALF), F32),
            pltpu.SemaphoreType.DMA((4,)),
        ],
        compiler_params=pltpu.CompilerParams(vmem_limit_bytes=16 << 20),
        name="prepare",
    )(in_hbm(u_basis), in_hbm(v_basis), in_hbm(ranks), in_hbm(singular.reshape(columns // HALF, HALF)))
    flip = [(0, 1), (1, 0)]
    turned, stack, sel, live = lax.optimization_barrier((turned, stack, sel, live))
    near = jnp.stack([turned, lax.ppermute(turned, "z4", flip)])
    near = jnp.concatenate([near, lax.ppermute(near, "z2", flip)])

    full = lax.all_to_all(stack, "y", 0, 0)
    full, near = lax.optimization_barrier((full, near))
    halves = [near, lax.ppermute(near, "z1", flip)]

    half = 3 * SIDE
    keep, give, right, saved_sel = pl.pallas_call(
        functools.partial(gram_kernel, rows_u),
        out_shape=(
            jax.ShapeDtypeStruct((half, HALF), F32),
            jax.ShapeDtypeStruct((half, HALF), BF),
            pltpu.HBM((rows_v, LIVE), BF),
            pltpu.HBM((columns, LIVE), BF),
        ),
        in_specs=[smem, smem, vmem, vmem],
        out_specs=(vmem, vmem, hbm, hbm),
        scratch_shapes=[
            pltpu.VMEM((rows_v, LIVE), BF),
            pltpu.VMEM((rows_u, LIVE), BF),
            pltpu.SemaphoreType.DMA((2,)),
        ],
        compiler_params=pltpu.CompilerParams(vmem_limit_bytes=24 << 20),
        cost_estimate=pl.CostEstimate(flops=1 << 30, bytes_accessed=4 << 20, transcendentals=0),
        name="gram",
    )(place.reshape(1), core.reshape(1), full, sel)

    mine = keep + lax.ppermute(give, "c", flip).astype(F32)
    spread = lax.all_to_all(mine.astype(BF).reshape(nx * nz, half // (nx * nz), HALF), ("x",) + Z, 0, 0)
    up = [(a, (a + 1) % nx) for a in range(nx)]
    down = [(b, a) for a, b in up]
    before = [lax.ppermute(h, "x", up) for h in halves]
    after = [lax.ppermute(h, "x", down) for h in halves]
    own = jnp.concatenate(halves)
    spread, own = lax.optimization_barrier((spread, own))
    piece = jnp.sum(spread.astype(F32), axis=0).astype(BF)

    piece = lax.all_to_all(jnp.broadcast_to(piece[None], (nz,) + piece.shape), Z, 0, 0)
    over = [(a, (a + 2) % nx) for a in range(nx)]
    across = [lax.ppermute(after[0], "x", down), lax.ppermute(halves[1], "x", over)]
    piece, before, after = lax.optimization_barrier((piece, before, after))
    parts = [own] + [p for h in range(2) for p in (before[h], after[h], across[h])]
    parts += [lax.ppermute(p, "c", flip) for p in parts]
    piece = piece.reshape(-1, HALF)
    piece = lax.all_to_all(jnp.broadcast_to(piece[None], (ny * nx,) + piece.shape), ("y", "x"), 0, 0)
    piece, parts = lax.optimization_barrier((piece, parts))
    piece = piece.reshape(ny, 3, SIDE, HALF)
    other = lax.ppermute(piece, "c", flip)

    rows = nz * nc * rows_u
    here = jnp.stack([lax.axis_index("x"), lax.axis_index(Z), core])
    out = pl.pallas_call(
        finish_kernel,
        out_shape=jax.ShapeDtypeStruct((rows_v, rows), BF),
        in_specs=[smem, vmem, vmem, hbm, vmem, hbm] + [hbm] * len(parts),
        out_specs=hbm,
        scratch_shapes=[pltpu.VMEM((LIVE, LIVE), BF)] * 6
        + [
            pltpu.VMEM((rows_v, LIVE), BF),
            pltpu.VMEM((columns, LIVE), BF),
            pltpu.VMEM((2 * rows_v, columns), BF),
            pltpu.VMEM((nx, nz, nc, rows_u, width), BF),
            pltpu.VMEM((rows_v, rows), BF),
            pltpu.SemaphoreType.DMA((2,)),
            pltpu.SemaphoreType.DMA((2, nc, 4)),
            pltpu.SemaphoreType.DMA((nz,)),
        ],
        compiler_params=pltpu.CompilerParams(vmem_limit_bytes=44 << 20),
        cost_estimate=pl.CostEstimate(flops=12 << 30, bytes_accessed=12 << 20, transcendentals=0),
        name="finish",
    )(here, piece, other, in_hbm(right), live, in_hbm(saved_sel), *[in_hbm(p) for p in parts])
    return out.T


def solution(mesh):
    grid = Mesh(mesh.devices.reshape(4, 4, 2, 2, 2, 2), ("y", "x") + Z + ("c",))
    row = ("x",) + Z + ("c",)
    return jax.shard_map(
        on_device,
        mesh=grid,
        in_specs=(P(row, "y"), P(row, "y"), P(), P()),
        out_specs=P("y", row),
        check_vma=False,
    )
```
